128 devices in a mesh: dp: 16 (over y, x_lo, core), fsdp: 8 (over z, x_hi).
Axes of the slice: x: 4 (x_hi: 2, x_lo: 2; x = x_hi * 2 + x_lo), y: 4, z: 4, core: 2. Of those that a mesh axis runs over, the one named last changes fastest.
Arguments:
- hidden: bfloat16 [1536, 28672], P('fsdp', 'dp'), may hold values from -6 to 6
- grad_out: bfloat16 [1536, 8192], P('fsdp', 'dp'), may hold values from -6 to 6
- weight: bfloat16 [28672, 8192], P('dp', 'fsdp'), may hold values from -0.0625 to 0.0625
- basis: bfloat16 [8192, 1024], P('fsdp'), may hold values from -0.1875 to 0.1875
- first_moment: float32 [1024, 28672], P('fsdp', 'dp'), may hold values from -60 to 60
- second_moment: float32 [1024, 28672], P('fsdp', 'dp'), may hold values from 1 to 100
Outputs:
- grad_hidden: bfloat16 [1536, 28672], P('fsdp', 'dp')
- update: bfloat16 [28672, 8192], P('dp', 'fsdp')
- new_first: float32 [1024, 28672], P('fsdp', 'dp')
- new_second: float32 [1024, 28672], P('fsdp', 'dp')
The draws below stay inside these ranges and needn't reach their ends.
All inputs are finite; a program needn't handle non-finite values.
Results may differ from the reference program's by a relative error of at most 0.025.
Values may be sent and summed in bfloat16 or wider, within the bound.
No kernel may reach another device: no remote copies, remote signals or barrier semaphores. Data moves between devices by JAX's collectives and lax.ppermute only.
A program may use at most 128 MiB of HBM per device.

```python
import math
import jax
import jax.numpy as jnp

D = 8192
FF = 28672
R = 1024
TOK = 192
TOKENS = 1536
N_FSDP = 8


def block_levels(rng, shape, cuts, low, high):
    level = 1.0
    for position, parts in cuts:
        heights = jax.random.uniform(jax.random.fold_in(jax.random.fold_in(rng, 6), position), (parts,), jnp.float32, low / len(cuts), high / len(cuts))
        level = level * jnp.repeat(jnp.exp(heights), shape[position] // parts).reshape((-1,) + (1,) * (len(shape) - 1 - position))
    return level


def noise(stream_key, shape, deviation, bound, pieces=(), dtype=jnp.bfloat16):
    loudness = block_levels(stream_key, shape, pieces, -0.22, 0.18) if pieces else 1.0
    values = jax.random.normal(stream_key, shape, jnp.float32) * deviation * loudness
    return jnp.minimum(jnp.maximum(values, -bound), bound).astype(dtype)


def setup_inputs(seed: int = 0) -> dict:
    streams_of = jax.random.split(jax.random.key(seed), 7)
    hidden = noise(streams_of[0], (TOKENS, FF), 1.0, 6.0, ((0, 8), (1, 16)))
    grad_out = noise(streams_of[1], (TOKENS, D), 1.0, 6.0, ((0, 8), (1, 16)))
    weight = noise(streams_of[2], (FF, D), D ** -0.5, 0.0625, ((0, 16), (1, 8)))
    basis = noise(streams_of[3], (D, R), R ** -0.5, 0.1875, ((0, 8),))
    first_moment = noise(streams_of[4], (R, FF), 10.0, 60.0, ((0, 8), (1, 16)), jnp.float32)
    second_moment = jnp.clip(jnp.exp(math.log(100.0) - 4.6051702 * jax.random.uniform(streams_of[5], (R, FF), jnp.float32) ** block_levels(streams_of[5], (R, FF), ((0, 8), (1, 16)), -0.2, 0.2)), 1.0, 100.0)
    return {"hidden": hidden, "grad_out": grad_out, "weight": weight, "basis": basis, "first_moment": first_moment, "second_moment": second_moment}


beta_one = 0.9
beta_two = 0.999
corr_one = 1.0 - 0.9 ** 10
corr_two = 1.0 - 0.999 ** 10
eps_adam = 1e-08
galore_scale = 0.25

def reference(hidden, grad_out, weight, basis, first_moment, second_moment):
    grad_hidden = jnp.dot(grad_out, weight.T, preferred_element_type=jnp.float32).astype(jnp.bfloat16)
    low_grad = jnp.dot(grad_out, basis, preferred_element_type=jnp.float32).astype(jnp.bfloat16)
    projected = jnp.zeros((R, FF), jnp.float32)
    for block in range(N_FSDP):
        rows_low = low_grad[block * TOK:(block + 1) * TOK]
        rows_hid = hidden[block * TOK:(block + 1) * TOK]
        part = jnp.dot(rows_low.T, rows_hid, preferred_element_type=jnp.float32).astype(jnp.bfloat16)
        projected = projected + part.astype(jnp.float32)
    new_first = beta_one * first_moment + (1.0 - beta_one) * projected
    new_second = beta_two * second_moment + (1.0 - beta_two) * projected * projected
    direction = (new_first / corr_one / (jnp.sqrt(new_second / corr_two) + eps_adam)).astype(jnp.bfloat16)
    update = (galore_scale * jnp.dot(direction.T, basis.T, preferred_element_type=jnp.float32)).astype(jnp.bfloat16)
    return (grad_hidden, update, new_first, new_second)
```

```python
import jax
import jax.numpy as jnp
from jax import lax
from jax.sharding import Mesh, PartitionSpec as P

beta_one = 0.9
beta_two = 0.999
corr_one = 1.0 - 0.9**10
corr_two = 1.0 - 0.999**10
eps_adam = 1e-08
galore_scale = 0.25

F32 = jnp.float32
BF16 = jnp.bfloat16


def ring(axis, step):
    pairs = [(i, (i + step) % 4) for i in range(4)]
    return lambda a: lax.ppermute(a, axis, pairs)


def swap(axis):
    return lambda a: lax.ppermute(a, axis, [(0, 1), (1, 0)])


z_up, z_down = ring("z", 1), ring("z", 3)
y_up, y_down, y_two = ring("y", 1), ring("y", 3), ring("y", 2)
x_far, x_near, core = swap("xh"), swap("xl"), swap("c")


def transpose_blocks(a):
    pairs = []
    for y in range(4):
        for xl in range(2):
            for z in range(4):
                for xh in range(2):
                    pairs.append((((y * 2 + xl) * 4 + z) * 2 + xh, ((z * 2 + xh) * 4 + y) * 2 + xl))
    return lax.ppermute(a, ("y", "xl", "z", "xh"), pairs)


def gather_tokens(a):
    other = x_near(a)
    same = lax.axis_index("xl") == lax.axis_index("xh")
    pair = jnp.concatenate([jnp.where(same, a, other), jnp.where(same, other, a)], axis=0)
    up, down, two = y_down(pair), y_up(pair), y_two(pair)
    return jnp.concatenate([pair, up, two, down], axis=0)


def token_block(a, i):
    y, z = lax.axis_index("y"), lax.axis_index("z")
    return lax.dynamic_slice_in_dim(a, ((z - y + i // 2) % 4 * 2 + i % 2) * 192, 192, axis=0)


def gather_start(a):
    return [a, x_far(a), z_up(a), z_down(a)]


def gather_end(a, x, below, above):
    half = a.shape[0] // 2
    first, second = z_up(below[:half]), z_down(above[half:])
    xbelow, xabove = z_up(x), z_down(x)
    two = jnp.concatenate([first, second], axis=0)
    xtwo = x_far(two)
    return [a, x, above, xabove, two, xtwo, below, xbelow]


def after(index, arrays):
    total = sum(a[0, 0].astype(F32) for a in arrays)
    return index + (total != total).astype(jnp.int32)


def dot(a, b, ca, cb):
    return lax.dot_general(a, b, (((ca,), (cb,)), ((), ())), preferred_element_type=F32)


def shards(hidden, grad_out, weight, basis, first_moment, second_moment):
    c, z, xh = (lax.axis_index(n) for n in ("c", "z", "xh"))
    t = transpose_blocks(grad_out)
    begun = gather_start(hidden)

    row = after(c, begun[1:]) * 512
    part = dot(t, lax.dynamic_slice_in_dim(basis, row, 512, axis=0), 1, 0).astype(BF16)
    part = part.reshape(192, 8, 128).transpose(1, 0, 2)
    part = lax.all_to_all(part, ("z", "xh"), 0, 0, tiled=True)
    mine = jnp.sum(part.astype(F32), axis=0).astype(BF16)
    mine = (mine.astype(F32) + core(mine).astype(F32)).astype(BF16)
    low = gather_tokens(mine)
    hidden_blocks = gather_end(*begun)

    half = gather_tokens(t)
    other = core(half)
    col = jnp.concatenate([jnp.where(c == 0, half, other), jnp.where(c == 0, other, half)], axis=1)

    def partial(i):
        return dot(token_block(col, i), weight, 1, 1)

    far = x_far(partial(5).astype(BF16))
    xsum_up, xsum_down = z_up(partial(3).astype(BF16)), z_down(partial(7).astype(BF16))
    two = (partial(4) + far.astype(F32)).astype(BF16)
    first, second = z_up(two[:96]), z_down(two[96:])
    up, down = partial(2), partial(6)
    up = jnp.concatenate([up[:96] + first.astype(F32), up[96:]], axis=0).astype(BF16)
    down = jnp.concatenate([down[:96], down[96:] + second.astype(F32)], axis=0).astype(BF16)
    up, down = z_up(up), z_down(down)
    xsum = (partial(1) + xsum_up.astype(F32) + xsum_down.astype(F32)).astype(BF16)
    xsum = x_far(xsum)
    grad_hidden = (partial(0) + up.astype(F32) + down.astype(F32) + xsum.astype(F32)).astype(BF16)

    projected = jnp.zeros((128, 1792), F32)
    for i, block in enumerate(hidden_blocks):
        projected = projected + dot(token_block(low, i), block, 0, 0).astype(BF16).astype(F32)

    new_first = beta_one * first_moment + (1.0 - beta_one) * projected
    new_second = beta_two * second_moment + (1.0 - beta_two) * projected * projected
    direction = (new_first / corr_one / (jnp.sqrt(new_second / corr_two) + eps_adam)).astype(BF16)

    ranks = jnp.zeros((1024, 1792), BF16)
    for i, block in enumerate(gather_end(*gather_start(direction))):
        place = (z + i // 2) % 4 * 2 + (xh + i % 2) % 2
        ranks = lax.dynamic_update_slice_in_dim(ranks, block, place * 128, axis=0)
    update = (galore_scale * dot(ranks, basis, 0, 1)).astype(BF16)
    return (grad_hidden, update, new_first, new_second)


def solution(mesh):
    fine = Mesh(mesh.devices.reshape(4, 2, 2, 4, 2), ("y", "xl", "c", "z", "xh"))
    fsdp, dp = ("z", "xh"), ("y", "xl", "c")
    return jax.shard_map(
        shards,
        mesh=fine,
        in_specs=(
            P(fsdp, dp),
            P(fsdp, dp),
            P(dp, fsdp),
            P(fsdp, None),
            P(fsdp, dp),
            P(fsdp, dp),
        ),
        out_specs=(P(fsdp, dp), P(dp, fsdp), P(fsdp, dp), P(fsdp, dp)),
        check_vma=False,
    )
```

```python
import jax
import jax.numpy as jnp
from jax import lax
from jax.sharding import Mesh, PartitionSpec as P

beta_one = 0.9
beta_two = 0.999
corr_one = 1.0 - 0.9**10
corr_two = 1.0 - 0.999**10
eps_adam = 1e-08
galore_scale = 0.25

F32 = jnp.float32
BF16 = jnp.bfloat16


def ring(axis, step):
    pairs = [(i, (i + step) % 4) for i in range(4)]
    return lambda a: lax.ppermute(a, axis, pairs)


def swap(axis):
    return lambda a: lax.ppermute(a, axis, [(0, 1), (1, 0)])


z_up, z_down = ring("z", 1), ring("z", 3)
z_two = ring("z", 2)
y_up, y_down, y_two = ring("y", 1), ring("y", 3), ring("y", 2)
x_far, x_near, core = swap("xh"), swap("xl"), swap("c")


def transpose_blocks(a):
    pairs = []
    for y in range(4):
        for xl in range(2):
            for z in range(4):
                for xh in range(2):
                    pairs.append((((y * 2 + xl) * 4 + z) * 2 + xh, ((z * 2 + xh) * 4 + y) * 2 + xl))
    return lax.ppermute(a, ("y", "xl", "z", "xh"), pairs)


def pair_tokens(a):
    other = x_near(a)
    same = lax.axis_index("xl") == lax.axis_index("xh")
    return jnp.concatenate([jnp.where(same, a, other), jnp.where(same, other, a)], axis=0)


def ring_tokens(pair):
    up, down, two = y_down(pair), y_up(pair), y_two(pair)
    return jnp.concatenate([pair, up, two, down], axis=0)


def token_block(a, i):
    y, z = lax.axis_index("y"), lax.axis_index("z")
    return lax.dynamic_slice_in_dim(a, ((z - y + i // 2) % 4 * 2 + i % 2) * 192, 192, axis=0)


def dot(a, b, ca, cb):
    return lax.dot_general(a, b, (((ca,), (cb,)), ((), ())), preferred_element_type=F32)


def shards(hidden, grad_out, weight, basis, first_moment, second_moment):
    c, z, xh = (lax.axis_index(n) for n in ("c", "z", "xh"))
    w_mine = lax.dynamic_slice_in_dim(weight, c * 512, 512, axis=1)
    w_other = lax.dynamic_slice_in_dim(weight, (1 - c) * 512, 512, axis=1)

    t = transpose_blocks(grad_out)
    hx, hbelow, habove = x_far(hidden), z_up(hidden), z_down(hidden)
    pair = pair_tokens(t)
    part = dot(t, lax.dynamic_slice_in_dim(basis, c * 512, 512, axis=0), 1, 0).astype(BF16)
    part = part.reshape(192, 8, 128).transpose(1, 0, 2)
    part, pair, hx, hbelow, habove = lax.optimization_barrier((part, pair, hx, hbelow, habove))

    hxbelow, hxabove = z_up(hx), z_down(hx)
    part = lax.all_to_all(part, ("z", "xh"), 0, 0, tiled=True)
    half = ring_tokens(pair)
    mine = jnp.sum(part.astype(F32), axis=0).astype(BF16)
    mine, half, hxbelow, hxabove = lax.optimization_barrier((mine, half, hxbelow, hxabove))
    hfirst, hsecond = z_up(hbelow[:96]), z_down(habove[96:])
    other = core(half)
    mine = (mine.astype(F32) + core(mine).astype(F32)).astype(BF16)
    mine = pair_tokens(mine)

    def partial(i):
        return dot(token_block(half, i), w_mine, 1, 1) + dot(token_block(other, i), w_other, 1, 1)

    xup, xdown = partial(3).astype(BF16), partial(7).astype(BF16)
    mine, xup, xdown, hfirst, hsecond = lax.optimization_barrier((mine, xup, xdown, hfirst, hsecond))
    xup, xdown = z_up(xup), z_down(xdown)
    far = x_far(partial(5).astype(BF16))
    htwo = jnp.concatenate([hfirst, hsecond], axis=0)
    hxtwo = x_far(htwo)
    low = ring_tokens(mine)
    low, far, xup, xdown = lax.optimization_barrier((low, far, xup, xdown))
    two = (partial(4) + far.astype(F32)).astype(BF16)
    first, second = z_up(two[:96]), z_down(two[96:])

    projected = jnp.zeros((128, 1792), F32)
    for i, block in enumerate([hidden, hx, habove, hxabove, htwo, hxtwo, hbelow, hxbelow]):
        projected = projected + dot(token_block(low, i), block, 0, 0).astype(BF16).astype(F32)
    new_first = beta_one * first_moment + (1.0 - beta_one) * projected
    new_second = beta_two * second_moment + (1.0 - beta_two) * projected * projected
    direction = (new_first / corr_one / (jnp.sqrt(new_second / corr_two) + eps_adam)).astype(BF16)

    direction, first, second = lax.optimization_barrier((direction, first, second))

    dx, dbelow, dabove, dtwo = x_far(direction), z_up(direction), z_down(direction), z_two(direction)
    dxbelow, dxabove, dxtwo = z_up(dx), z_down(dx), x_far(dtwo)

    def columns(side):
        starts = [(((z + r) % 4) * 2 + side) * 128 for r in range(4)]
        return jnp.concatenate([lax.dynamic_slice_in_dim(basis, s, 128, axis=1) for s in starts], axis=1)

    expanded = dot(jnp.concatenate([direction, dabove, dtwo, dbelow], axis=0), columns(xh), 0, 1)
    expanded += dot(jnp.concatenate([dx, dxabove, dxtwo, dxbelow], axis=0), columns(1 - xh), 0, 1)
    update = (galore_scale * expanded).astype(BF16)

    up, down = partial(2), partial(6)
    up = jnp.concatenate([up[:96] + first.astype(F32), up[96:]], axis=0).astype(BF16)
    down = jnp.concatenate([down[:96], down[96:] + second.astype(F32)], axis=0).astype(BF16)
    up, down = z_up(up), z_down(down)
    xsum = x_far((partial(1) + xup.astype(F32) + xdown.astype(F32)).astype(BF16))
    grad_hidden = (partial(0) + up.astype(F32) + down.astype(F32) + xsum.astype(F32)).astype(BF16)
    return (grad_hidden, update, new_first, new_second)


def solution(mesh):
    fine = Mesh(mesh.devices.reshape(4, 2, 2, 4, 2), ("y", "xl", "c", "z", "xh"))
    fsdp, dp = ("z", "xh"), ("y", "xl", "c")
    return jax.shard_map(
        shards,
        mesh=fine,
        in_specs=(
            P(fsdp, dp),
            P(fsdp, dp),
            P(dp, fsdp),
            P(fsdp, None),
            P(fsdp, dp),
            P(fsdp, dp),
        ),
        out_specs=(P(fsdp, dp), P(dp, fsdp), P(fsdp, dp), P(fsdp, dp)),
        check_vma=False,
    )
```

```python
import jax
import jax.numpy as jnp
from jax import lax
from jax.sharding import Mesh, PartitionSpec as P

beta_one = 0.9
beta_two = 0.999
corr_one = 1.0 - 0.9**10
corr_two = 1.0 - 0.999**10
eps_adam = 1e-08
galore_scale = 0.25

F32 = jnp.float32
BF16 = jnp.bfloat16


def ring(axis, step):
    pairs = [(i, (i + step) % 4) for i in range(4)]
    return lambda a: lax.ppermute(a, axis, pairs)


def swap(axis):
    return lambda a: lax.ppermute(a, axis, [(0, 1), (1, 0)])


z_up, z_down = ring("z", 1), ring("z", 3)
z_two = ring("z", 2)
y_up, y_down, y_two = ring("y", 1), ring("y", 3), ring("y", 2)
x_far, x_near, core = swap("xh"), swap("xl"), swap("c")


def transpose_blocks(a):
    pairs = []
    for y in range(4):
        for xl in range(2):
            for z in range(4):
                for xh in range(2):
                    pairs.append((((y * 2 + xl) * 4 + z) * 2 + xh, ((z * 2 + xh) * 4 + y) * 2 + xl))
    return lax.ppermute(a, ("y", "xl", "z", "xh"), pairs)


def pair_tokens(a):
    other = x_near(a)
    same = lax.axis_index("xl") == lax.axis_index("xh")
    return jnp.concatenate([jnp.where(same, a, other), jnp.where(same, other, a)], axis=0)


def ring_tokens(pair):
    up, down, two = y_down(pair), y_up(pair), y_two(pair)
    return jnp.concatenate([pair, up, two, down], axis=0)


def token_block(a, i):
    y, z = lax.axis_index("y"), lax.axis_index("z")
    return lax.dynamic_slice_in_dim(a, ((z - y + i // 2) % 4 * 2 + i % 2) * 192, 192, axis=0)


def dot(a, b, ca, cb):
    return lax.dot_general(a, b, (((ca,), (cb,)), ((), ())), preferred_element_type=F32)


def shards(hidden, grad_out, weight, basis, first_moment, second_moment):
    c, z, xh = (lax.axis_index(n) for n in ("c", "z", "xh"))
    halves = [lax.dynamic_slice_in_dim(weight, k * 512, 512, axis=1) for k in (c, 1 - c)]
    turned = jnp.concatenate(halves, axis=1)

    t = transpose_blocks(grad_out)
    hx, hbelow, habove = x_far(hidden), z_up(hidden), z_down(hidden)
    pair = pair_tokens(t)
    part = dot(t, lax.dynamic_slice_in_dim(basis, c * 512, 512, axis=0), 1, 0).astype(BF16)
    part = part.reshape(192, 8, 128).transpose(1, 0, 2)
    part, pair, hx, hbelow, habove = lax.optimization_barrier((part, pair, hx, hbelow, habove))

    hxbelow, hxabove = z_up(hx), z_down(hx)
    part = lax.all_to_all(part, ("z", "xh"), 0, 0, tiled=True)
    half = ring_tokens(pair)
    mine = jnp.sum(part.astype(F32), axis=0).astype(BF16)
    mine, half, hxbelow, hxabove = lax.optimization_barrier((mine, half, hxbelow, hxabove))
    hfirst = z_up(jnp.concatenate([hbelow[:96], hxbelow[:96]], axis=0))
    hsecond = z_down(jnp.concatenate([habove[96:], hxabove[96:]], axis=0))
    other = core(half)
    mine = (mine.astype(F32) + core(mine).astype(F32)).astype(BF16)
    mine = pair_tokens(mine)

    sums = dot(jnp.concatenate([half, other], axis=1), turned, 1, 1).astype(BF16)

    def partial(i):
        return token_block(sums, i)

    xup, xdown = partial(3), partial(7)
    mine, xup, xdown, hfirst, hsecond = lax.optimization_barrier((mine, xup, xdown, hfirst, hsecond))
    xup, xdown = z_up(xup), z_down(xdown)
    far = x_far(partial(5))
    htwo = jnp.concatenate([hfirst[:96], hsecond[:96]], axis=0)
    hxtwo = jnp.concatenate([hfirst[96:], hsecond[96:]], axis=0)
    low = ring_tokens(mine)
    far, xup, xdown = lax.optimization_barrier((far, xup, xdown))
    two = (partial(4).astype(F32) + far.astype(F32)).astype(BF16)
    first, second = z_up(two[:96]), z_down(two[96:])

    projected = jnp.zeros((128, 1792), F32)
    for i, block in enumerate([hidden, hx, habove, hxabove, htwo, hxtwo, hbelow, hxbelow]):
        projected = projected + dot(token_block(low, i), block, 0, 0).astype(BF16).astype(F32)
    new_first = beta_one * first_moment + (1.0 - beta_one) * projected
    new_second = beta_two * second_moment + (1.0 - beta_two) * projected * projected
    direction = (new_first / corr_one / (jnp.sqrt(new_second / corr_two) + eps_adam)).astype(BF16)

    direction, first, second = lax.optimization_barrier((direction, first, second))

    dx, dbelow, dabove, dtwo = x_far(direction), z_up(direction), z_down(direction), z_two(direction)
    dxbelow, dxabove, dxtwo = z_up(dx), z_down(dx), x_far(dtwo)

    def columns(side):
        starts = [(((z + r) % 4) * 2 + side) * 128 for r in range(4)]
        return jnp.concatenate([lax.dynamic_slice_in_dim(basis, s, 128, axis=1) for s in starts], axis=1)

    expanded = dot(jnp.concatenate([direction, dabove, dtwo, dbelow], axis=0), columns(xh), 0, 1)
    expanded += dot(jnp.concatenate([dx, dxabove, dxtwo, dxbelow], axis=0), columns(1 - xh), 0, 1)
    update = (galore_scale * expanded).astype(BF16)

    up, down = partial(2).astype(F32), partial(6).astype(F32)
    up = jnp.concatenate([up[:96] + first.astype(F32), up[96:]], axis=0).astype(BF16)
    down = jnp.concatenate([down[:96], down[96:] + second.astype(F32)], axis=0).astype(BF16)
    up, down = z_up(up), z_down(down)
    xsum = x_far((partial(1).astype(F32) + xup.astype(F32) + xdown.astype(F32)).astype(BF16))
    grad_hidden = (partial(0).astype(F32) + up.astype(F32) + down.astype(F32) + xsum.astype(F32)).astype(BF16)
    return (grad_hidden, update, new_first, new_second)


def solution(mesh):
    fine = Mesh(mesh.devices.reshape(4, 2, 2, 4, 2), ("y", "xl", "c", "z", "xh"))
    fsdp, dp = ("z", "xh"), ("y", "xl", "c")
    return jax.shard_map(
        shards,
        mesh=fine,
        in_specs=(
            P(fsdp, dp),
            P(fsdp, dp),
            P(dp, fsdp),
            P(fsdp, None),
            P(fsdp, dp),
            P(fsdp, dp),
        ),
        out_specs=(P(fsdp, dp), P(dp, fsdp), P(fsdp, dp), P(fsdp, dp)),
        check_vma=False,
    )
```

```python
import jax
import jax.numpy as jnp
from jax import lax
from jax.sharding import Mesh, PartitionSpec as P

beta_one = 0.9
beta_two = 0.999
corr_one = 1.0 - 0.9**10
corr_two = 1.0 - 0.999**10
eps_adam = 1e-08
galore_scale = 0.25

F32 = jnp.float32
BF16 = jnp.bfloat16


def ring(axis, step):
    pairs = [(i, (i + step) % 4) for i in range(4)]
    return lambda a: lax.ppermute(a, axis, pairs)


def swap(axis):
    return lambda a: lax.ppermute(a, axis, [(0, 1), (1, 0)])


z_up, z_down = ring("z", 1), ring("z", 3)
z_two = ring("z", 2)
y_up, y_down, y_two = ring("y", 1), ring("y", 3), ring("y", 2)
x_far, x_near, core = swap("xh"), swap("xl"), swap("c")


def transpose_blocks(a):
    pairs = []
    for y in range(4):
        for xl in range(2):
            for z in range(4):
                for xh in range(2):
                    pairs.append((((y * 2 + xl) * 4 + z) * 2 + xh, ((z * 2 + xh) * 4 + y) * 2 + xl))
    return lax.ppermute(a, ("y", "xl", "z", "xh"), pairs)


def pair_tokens(a):
    other = x_near(a)
    same = lax.axis_index("xl") == lax.axis_index("xh")
    return jnp.concatenate([jnp.where(same, a, other), jnp.where(same, other, a)], axis=0)


def ring_tokens(pair):
    up, down, two = y_down(pair), y_up(pair), y_two(pair)
    return jnp.concatenate([pair, up, two, down], axis=0)


def token_block(a, i):
    y, z = lax.axis_index("y"), lax.axis_index("z")
    return lax.dynamic_slice_in_dim(a, ((z - y + i // 2) % 4 * 2 + i % 2) * 192, 192, axis=0)


def dot(a, b, ca, cb):
    return lax.dot_general(a, b, (((ca,), (cb,)), ((), ())), preferred_element_type=F32)


def shards(hidden, grad_out, weight, basis, first_moment, second_moment):
    c, z, xh = (lax.axis_index(n) for n in ("c", "z", "xh"))
    halves = [lax.dynamic_slice_in_dim(weight, k * 512, 512, axis=1) for k in (c, 1 - c)]
    turned = jnp.concatenate(halves, axis=1)

    t = transpose_blocks(grad_out)
    hx, hbelow, habove = x_far(hidden), z_up(hidden), z_down(hidden)
    pair = pair_tokens(t)
    part = dot(t, lax.dynamic_slice_in_dim(basis, c * 512, 512, axis=0), 1, 0).astype(BF16)
    part = part.reshape(192, 8, 128).transpose(1, 0, 2)
    part, pair, hx, hbelow, habove = lax.optimization_barrier((part, pair, hx, hbelow, habove))

    hxbelow, hxabove = z_up(hx), z_down(hx)
    part = lax.all_to_all(part, ("z", "xh"), 0, 0, tiled=True)
    half = ring_tokens(pair)
    mine = jnp.sum(part.astype(F32), axis=0).astype(BF16)
    mine, half, hxbelow, hxabove = lax.optimization_barrier((mine, half, hxbelow, hxabove))
    hfirst = z_up(jnp.concatenate([hbelow[:96], hxbelow[:96]], axis=0))
    hsecond = z_down(jnp.concatenate([habove[96:], hxabove[96:]], axis=0))
    other = core(half)
    mine = (mine.astype(F32) + core(mine).astype(F32)).astype(BF16)
    mine = pair_tokens(mine)

    sums = dot(jnp.concatenate([half, other], axis=1), turned, 1, 1).astype(BF16)

    def partial(i):
        return token_block(sums, i)

    xup, xdown = partial(3), partial(7)
    xup, xdown, hfirst, hsecond = lax.optimization_barrier((xup, xdown, hfirst, hsecond))
    xup, xdown = z_up(xup), z_down(xdown)
    far = x_far(partial(5))
    htwo = jnp.concatenate([hfirst[:96], hsecond[:96]], axis=0)
    hxtwo = jnp.concatenate([hfirst[96:], hsecond[96:]], axis=0)
    low = ring_tokens(mine)
    far, xup, xdown = lax.optimization_barrier((far, xup, xdown))
    two = (partial(4).astype(F32) + far.astype(F32)).astype(BF16)
    first, second = z_up(two[:96]), z_down(two[96:])

    projected = jnp.zeros((128, 1792), F32)
    for i, block in enumerate([hidden, hx, habove, hxabove, htwo, hxtwo, hbelow, hxbelow]):
        projected = projected + dot(token_block(low, i), block, 0, 0).astype(BF16).astype(F32)
    new_first = beta_one * first_moment + (1.0 - beta_one) * projected
    new_second = beta_two * second_moment + (1.0 - beta_two) * projected * projected
    direction = (new_first / corr_one / (jnp.sqrt(new_second / corr_two) + eps_adam)).astype(BF16)

    direction, first, second = lax.optimization_barrier((direction, first, second))

    dx, dbelow, dabove, dtwo = x_far(direction), z_up(direction), z_down(direction), z_two(direction)
    dxbelow, dxabove, dxtwo = z_up(dx), z_down(dx), x_far(dtwo)

    def columns(side):
        starts = [(((z + r) % 4) * 2 + side) * 128 for r in range(4)]
        return jnp.concatenate([lax.dynamic_slice_in_dim(basis, s, 128, axis=1) for s in starts], axis=1)

    expanded = dot(jnp.concatenate([direction, dabove, dtwo, dbelow], axis=0), columns(xh), 0, 1)
    expanded += dot(jnp.concatenate([dx, dxabove, dxtwo, dxbelow], axis=0), columns(1 - xh), 0, 1)
    update = (galore_scale * expanded).astype(BF16)

    up, down = partial(2).astype(F32), partial(6).astype(F32)
    up = jnp.concatenate([up[:96] + first.astype(F32), up[96:]], axis=0).astype(BF16)
    down = jnp.concatenate([down[:96], down[96:] + second.astype(F32)], axis=0).astype(BF16)
    up, down = z_up(up), z_down(down)
    xsum = x_far((partial(1).astype(F32) + xup.astype(F32) + xdown.astype(F32)).astype(BF16))
    grad_hidden = (partial(0).astype(F32) + up.astype(F32) + down.astype(F32) + xsum.astype(F32)).astype(BF16)
    return (grad_hidden, update, new_first, new_second)


def solution(mesh):
    fine = Mesh(mesh.devices.reshape(4, 2, 2, 4, 2), ("y", "xl", "c", "z", "xh"))
    fsdp, dp = ("z", "xh"), ("y", "xl", "c")
    return jax.shard_map(
        shards,
        mesh=fine,
        in_specs=(
            P(fsdp, dp),
            P(fsdp, dp),
            P(dp, fsdp),
            P(fsdp, None),
            P(fsdp, dp),
            P(fsdp, dp),
        ),
        out_specs=(P(fsdp, dp), P(dp, fsdp), P(fsdp, dp), P(fsdp, dp)),
        check_vma=False,
    )
```
